32 devices in a mesh: groups: 2 (over x), lat: 8 (over z, y), layer: 2 (over core).
Axes of the slice: x: 2, y: 2, z: 4, core: 2. Of those that a mesh axis runs over, the one named last changes fastest.
Arguments:
- streams: bfloat16 [2, 1024, 4096], P('layer', ('groups', 'lat')), parts along dimension 1, may hold values from -6 to 6
- enc_weight: bfloat16 [4, 4096, 8192], P(('groups', 'layer'), None, 'lat'), parts along dimension 0, may hold values from -0.0625 to 0.0625
- enc_bias: float32 [16384], P(('groups', 'lat')), parts along dimension 0, may hold values from -3 to 3
- dec_weight: bfloat16 [4, 8192, 4096], P(('groups', 'layer'), 'lat'), parts along dimension 0, may hold values from -0.198873782 to 0.198873782
- dec_bias: float32 [4, 4096], P(('groups', 'layer'), 'lat'), parts along dimension 0, may hold values from -3 to 3
Outputs:
- enc_grad: bfloat16 [4, 4096, 8192], P(('groups', 'layer'), None, 'lat'), parts along dimension 0
- enc_bias_grad: float32 [16384], P(('groups', 'lat')), parts along dimension 0
- dec_grad: bfloat16 [4, 8192, 4096], P(('groups', 'layer'), 'lat'), parts along dimension 0
- dec_bias_grad: float32 [4, 4096], P(('groups', 'layer'), 'lat'), parts along dimension 0
The draws below stay inside these ranges and needn't reach their ends.
There are 2 independent parts, one for each index of `groups`. The reference program is written for one: setup_inputs(seed, part) draws one part's arguments, and reference() takes and returns one part's arrays. A program takes and returns all parts, laid end to end along the dimension named above; each array names one. Nothing has to cross between parts.
All inputs are finite; a program needn't handle non-finite values.
Results may differ from the reference program's by a relative error of at most 0.0055.
Values may be sent and summed in bfloat16 or wider, within the bound.
A program may use at most 128 MiB of HBM per device.

```python
import jax
import jax.numpy as jnp
from jax import lax

D = 4096
H = 8192
ROWS = 512
LAYERS = 2


def draw_dec_weight(key, part):
    key = jax.random.fold_in(key, 7)
    first_key, second_key, third_key = jax.random.split(key, 3)
    base = jnp.clip(jax.random.normal(first_key, (LAYERS, H, D), jnp.float32), -3.0, 3.0)
    low_row, high_row = (0.3, 3.0)
    row_scale = jnp.exp(jax.random.uniform(second_key, (LAYERS, H, 1), jnp.float32, jnp.log(low_row), jnp.log(high_row)))
    col_scale = jnp.exp(jax.random.uniform(third_key, (1, 1, D), jnp.float32, jnp.log(0.5), jnp.log(2.0)))
    return (base * row_scale * col_scale / jnp.sqrt(jnp.float32(H))).astype(jnp.bfloat16)


def shard_levels(stream_key, dims, pieces, low, high):
    def one(position, shards_of):
        draws = jax.random.uniform(jax.random.fold_in(jax.random.fold_in(stream_key, 6), position), (shards_of,), jnp.float32, low / len(pieces), high / len(pieces))
        return jnp.repeat(jnp.exp(draws), dims[position] // shards_of).reshape((-1,) + (1,) * (len(dims) - position - 1))

    factor_of = one(*pieces[0])
    for cut in pieces[1:]:
        factor_of = factor_of * one(*cut)
    return factor_of


def normal_values(stream_key, shape, deviation, bound, pieces=(), kind=jnp.bfloat16):
    gain = shard_levels(stream_key, shape, pieces, -0.22, 0.18) if pieces else 1.0
    entries = jax.random.normal(stream_key, shape, jnp.float32) * deviation * gain
    return jnp.minimum(jnp.maximum(entries, -bound), bound).astype(kind)


def setup_inputs(seed: int = 0, part: int = 0) -> dict:
    streams_of = jax.random.split(jax.random.key(seed), 6)
    part_splits = jax.random.split(jax.random.fold_in(streams_of[5], part), 6)
    streams = normal_values(part_splits[0], (LAYERS, ROWS, D), 1.0, 6.0, ((0, 2), (1, 8)))
    enc_weight = normal_values(part_splits[1], (LAYERS, D, H), (LAYERS * D) ** -0.5, 0.0625, ((0, 2), (2, 8)))
    enc_bias = normal_values(part_splits[2], (H,), 0.5, 3.0, ((0, 8),), jnp.float32)
    dec_weight = draw_dec_weight(jax.random.fold_in(jax.random.fold_in(streams_of[5], part), 71), part)
    dec_bias = normal_values(part_splits[4], (LAYERS, D), 0.5, 3.0, ((0, 2), (1, 8)), jnp.float32)
    return {"streams": streams, "enc_weight": enc_weight, "enc_bias": enc_bias, "dec_weight": dec_weight, "dec_bias": dec_bias}


penalty_weight = 1.0
epsilon_sq = 1e-06

def reference(streams, enc_weight, enc_bias, dec_weight, dec_bias):
    pre = jnp.zeros((ROWS, H), jnp.float32)
    for layer_idx in range(LAYERS):
        pre = pre + jnp.dot(streams[layer_idx], enc_weight[layer_idx], preferred_element_type=jnp.float32)
    pre = pre + enc_bias
    features = jax.nn.softplus(pre).astype(jnp.bfloat16)
    row_norm = jnp.sqrt(lax.optimization_barrier(jnp.sum(jnp.square(dec_weight.astype(jnp.float32)), axis=2)) + epsilon_sq)
    strength = lax.optimization_barrier(jnp.sum(row_norm, axis=0))
    row_scale = 1.0 / jnp.sqrt(jnp.float32(ROWS))
    feat_sums = lax.optimization_barrier(jnp.sum(features.astype(jnp.float32), axis=0))
    feat_grad = jnp.zeros((ROWS, H), jnp.float32)
    dec_grads = []
    bias_grads = []
    for layer_idx in range(LAYERS):
        recon = jnp.dot(features, dec_weight[layer_idx], preferred_element_type=jnp.float32)
        recon_err = recon + dec_bias[layer_idx] - streams[layer_idx].astype(jnp.float32)
        err_grad = recon_err * row_scale
        bias_grads.append(lax.optimization_barrier(jnp.sum(err_grad, axis=0)))
        err_round = err_grad.astype(jnp.bfloat16)
        direct = jnp.dot(features.T, err_round, preferred_element_type=jnp.float32)
        shrink = (penalty_weight * row_scale * feat_sums / row_norm[layer_idx])[:, None] * dec_weight[layer_idx].astype(jnp.float32)
        dec_grads.append((direct + shrink).astype(jnp.bfloat16))
        feat_grad = feat_grad + jnp.dot(err_round, dec_weight[layer_idx].T, preferred_element_type=jnp.float32)
    feat_grad = feat_grad + penalty_weight * row_scale * strength
    pre_grad = feat_grad * jax.nn.sigmoid(pre)
    enc_bias_grad = lax.optimization_barrier(jnp.sum(pre_grad, axis=0))
    pre_round = pre_grad.astype(jnp.bfloat16)
    enc_grads = []
    for layer_idx in range(LAYERS):
        enc_grads.append(jnp.dot(streams[layer_idx].T, pre_round, preferred_element_type=jnp.float32).astype(jnp.bfloat16))
    return (jnp.stack(enc_grads), enc_bias_grad, jnp.stack(dec_grads), jnp.stack(bias_grads))
```

```python
import functools

import jax
import jax.numpy as jnp
from jax import lax
from jax.experimental import pallas as pl
from jax.experimental.pallas import tpu as pltpu
from jax.sharding import PartitionSpec as P

penalty_weight = 1.0
epsilon_sq = 1e-06
MESH = pl.DeviceIdType.MESH
MIB = 1024 * 1024
F32 = jnp.float32
BF16 = jnp.bfloat16


def ring_neighbours(n):
    index = lax.axis_index("lat")
    if n != 8:
        return lax.rem(index + 1, n), lax.rem(index + n - 1, n)
    half = n // 2

    def place_of(i):
        z, y = i // 2, lax.rem(i, 2)
        return jnp.where(y == 0, z, n - 1 - z)

    def index_of(p):
        return jnp.where(p < half, 2 * p, 2 * (n - 1 - p) + 1)

    place = place_of(index)
    return index_of(lax.rem(place + 1, n)), index_of(lax.rem(place + n - 1, n))


def step_kernel(
    n, x_ref, enc_hbm, enc_bias_ref, dec_hbm, dec_bias_ref, norm_ref,
    full_out, feat_out, err_out, round_out, bias_grad_ref, dec_bias_grad_ref,
    enc, dec, full, part, part_in, pre, feat, partial, sum_right, sum_left, in_right, in_left,
    err, grad, grad_in, rounded, norm_in,
    g_send, g_recv, r_send, r_recv, e_send, e_recv, p_send, p_recv, q_send, q_recv, n_sem, w_sem, o_sem,
):
    rows, width = x_ref.shape
    latents = enc.shape[1]
    half = n // 2
    hw = width // 2
    total = n * rows
    scale = float(1.0 / (total ** 0.5))
    right, left = ring_neighbours(n)
    other = 1 - lax.axis_index("layer")
    lat = lax.axis_index("lat")
    to_right, to_left, to_other = {"lat": right}, {"lat": left}, {"layer": other}
    sending = []

    load_enc = pltpu.make_async_copy(enc_hbm, enc, w_sem.at[0])
    load_dec = pltpu.make_async_copy(dec_hbm, dec, w_sem.at[1])
    load_enc.start()
    load_dec.start()

    barrier = pltpu.get_barrier_semaphore()
    for target in (to_right, to_left, to_other):
        pl.semaphore_signal(barrier, inc=1, device_id=target, device_id_type=MESH)

    def slot_rows(slot, count=1):
        return pl.ds(slot * rows, count * rows)

    def send(src, dst, s_sem, r_sem, target):
        copy = pltpu.make_async_remote_copy(
            src_ref=src, dst_ref=dst, send_sem=s_sem, recv_sem=r_sem,
            device_id=target, device_id_type=MESH,
        )
        copy.start()
        sending.append(copy)
        return copy

    def step_span(d):
        if d == 0:
            return 0, 1
        if d == half:
            return n - 1, 1
        return 2 * d - 1, 2

    def gather(buf, s_sem, r_sem, consume):
        got = {}

        def forward(d, h, way):
            if d > half or (d == half and h != way):
                return
            if way == 0:
                src = 0 if d == 1 else 2 * d - 3
                dst = n - 1 if d == half else 2 * d - 1
            else:
                src = 2 * (d - 1)
                dst = n - 1 if d == half else 2 * d
            cols = pl.ds(h * hw, hw)
            got[(d, h, way)] = send(
                buf.at[slot_rows(src), cols], buf.at[slot_rows(dst), cols],
                s_sem.at[way, d - 1, h], r_sem.at[way, d - 1, h],
                to_right if way == 0 else to_left,
            )

        for order in range(2):
            for way in range(2):
                forward(1, (order + way) % 2, way)
        consume(0)
        for d in range(1, half + 1):
            for order in range(2):
                for way in range(2):
                    h = (order + way) % 2
                    if (d, h, way) in got:
                        got[(d, h, way)].wait_recv()
                        forward(d + 1, h, way)
            consume(d)

    full[slot_rows(0), :] = x_ref[...]
    pl.semaphore_wait(barrier, 3)
    swap_norm = send(norm_ref, norm_in, n_sem.at[0], n_sem.at[1], to_other)

    tile = min(256, latents)
    swaps = {}

    def finish_pre(d):
        slot, count = step_span(d)
        swaps[d].wait_recv()

        @pl.loop(0, count * rows // 16)
        def _(i):
            r = pl.ds(pl.multiple_of(slot * rows + i * 16, 16), 16)
            value = part[r, :] + part_in[r, :] + enc_bias_ref[...]
            pre[r, :] = value
            soft = jnp.maximum(value, 0.0) + jnp.log1p(jnp.exp(-jnp.abs(value)))
            feat[r, :] = soft.astype(BF16)

    def encode(d):
        if d == 0:
            load_enc.wait()
        slot, count = step_span(d)
        r = slot_rows(slot, count)

        @pl.loop(0, latents // tile)
        def _(j):
            c = pl.ds(pl.multiple_of(j * tile, tile), tile)
            part[r, c] = jnp.dot(full[r, :], enc[:, c], preferred_element_type=F32)

        swaps[d] = send(part.at[r, :], part_in.at[r, :], p_send.at[d], p_recv.at[d], to_other)
        if d >= 1:
            finish_pre(d - 1)

    gather(full, g_send, g_recv, encode)
    save_full = pltpu.make_async_copy(full, full_out, o_sem.at[0])
    save_full.start()
    finish_pre(half)
    save_feat = pltpu.make_async_copy(feat, feat_out, o_sem.at[1])
    save_feat.start()

    load_dec.wait()
    wide = min(512, width)
    own = width // n

    def decode(d):
        slot, count = step_span(d)
        r = slot_rows(slot, count)
        to = pl.ds(0, count * rows)

        @pl.loop(0, width // wide)
        def _(j):
            c = pl.ds(pl.multiple_of(j * wide, wide), wide)
            partial[to, c] = jnp.dot(feat[r, :], dec[:, c], preferred_element_type=F32)

        mine = pl.ds(pl.multiple_of(lat * own, own), own)
        partial[to, mine] = partial[to, mine] + dec_bias_ref[...]

    def merge(source, base, arrived, index, target, h):
        @pl.loop(0, rows // 16)
        def _(i):
            r = pl.ds(pl.multiple_of(i * 16, 16), 16)
            c = pl.ds(h * hw, hw)
            value = source[pl.ds(pl.multiple_of(base + i * 16, 16), 16), c]
            if arrived is not None:
                value = value + arrived[index, r, c].astype(F32)
            target[r, c] = value.astype(target.dtype)

    moving = {}
    for d in range(half, 0, -1):
        decode(d)
        for order in range(2):
            for way in range(2):
                h = (order + way) % 2
                if d == half and h != way:
                    continue
                base = 0 if d == half or way == 1 else rows
                out = (sum_right, sum_left)[way]
                arrive = (in_right, in_left)[way]
                before = moving.get((d + 1, h, way))
                if before is not None:
                    before.wait_recv()
                merge(partial, base, None if before is None else arrive, d, out.at[d - 1], h)
                c = pl.ds(h * hw, hw)
                moving[(d, h, way)] = send(
                    out.at[d - 1, :, c], arrive.at[d - 1, :, c],
                    r_send.at[way, d - 1, h], r_recv.at[way, d - 1, h],
                    to_right if way == 0 else to_left,
                )
    decode(0)
    for order in range(2):
        for way in range(2):
            moving[(1, (order + way) % 2, way)].wait_recv()

    @pl.loop(0, rows // 16)
    def _(i):
        r = pl.ds(pl.multiple_of(i * 16, 16), 16)
        for h in range(2):
            c = pl.ds(h * hw, hw)
            recon = partial[r, c] + in_right[0, r, c].astype(F32) + in_left[0, r, c].astype(F32)
            err[r, c] = ((recon - x_ref[r, c].astype(F32)) * scale).astype(BF16)

    swap_norm.wait_recv()
    bias_grad_ref[...] = jnp.zeros_like(bias_grad_ref)
    grad_swaps = {}

    def finish_grad(d):
        slot, count = step_span(d)
        grad_swaps[d].wait_recv()

        @pl.loop(0, count * rows // 16)
        def _(i):
            r = pl.ds(pl.multiple_of(slot * rows + i * 16, 16), 16)
            strength = norm_ref[0:1, :] + norm_in[0:1, :]
            value = grad[r, :] + grad_in[r, :] + (penalty_weight * scale) * strength
            value = value * jax.nn.sigmoid(pre[r, :])
            rounded[r, :] = value.astype(BF16)
            bias_grad_ref[...] += jnp.sum(value, axis=0, keepdims=True)

    def decode_grad(d):
        slot, count = step_span(d)
        r = slot_rows(slot, count)

        @pl.loop(0, latents // tile)
        def _(j):
            c = pl.ds(pl.multiple_of(j * tile, tile), tile)
            grad[r, c] = lax.dot_general(
                err[r, :], dec[c, :], (((1,), (1,)), ((), ())), preferred_element_type=F32
            )

        grad_swaps[d] = send(grad.at[r, :], grad_in.at[r, :], q_send.at[d], q_recv.at[d], to_other)
        if d >= 1:
            finish_grad(d - 1)

    gather(err, e_send, e_recv, decode_grad)
    save_err = pltpu.make_async_copy(err, err_out, o_sem.at[2])
    save_err.start()
    mine = pl.ds(pl.multiple_of(lat * own, own), own)
    dec_bias_grad_ref[...] = jnp.zeros_like(dec_bias_grad_ref)

    @pl.loop(0, total // 64)
    def _(i):
        r = pl.ds(pl.multiple_of(i * 64, 64), 64)
        dec_bias_grad_ref[...] += jnp.sum(err[r, mine].astype(F32), axis=0, keepdims=True)

    finish_grad(half)
    save_round = pltpu.make_async_copy(rounded, round_out, o_sem.at[3])
    save_round.start()
    for copy in sending:
        copy.wait_send()
    for save in (save_full, save_feat, save_err, save_round):
        save.wait()


def main_call(n, x, enc, enc_bias, dec, dec_bias, norm):
    rows, width = x.shape
    latents = enc.shape[1]
    total = n * rows
    half = n // 2
    vmem = pl.BlockSpec(memory_space=pltpu.VMEM)
    hbm = pl.BlockSpec(memory_space=pl.ANY)
    dma = pltpu.SemaphoreType.DMA
    steps = dma((2, half, 2))
    swap = dma((half + 1,))
    return pl.pallas_call(
        functools.partial(step_kernel, n),
        out_shape=(
            jax.ShapeDtypeStruct((total, width), BF16),
            jax.ShapeDtypeStruct((total, latents), BF16),
            jax.ShapeDtypeStruct((total, width), BF16),
            jax.ShapeDtypeStruct((total, latents), BF16),
            jax.ShapeDtypeStruct((1, latents), F32),
            jax.ShapeDtypeStruct((1, width // n), F32),
        ),
        in_specs=[vmem, hbm, vmem, hbm, vmem, vmem],
        out_specs=(hbm, hbm, hbm, hbm, vmem, vmem),
        scratch_shapes=[
            pltpu.VMEM((width, latents), BF16),
            pltpu.VMEM((latents, width), BF16),
            pltpu.VMEM((total, width), BF16),
            pltpu.VMEM((total, latents), F32),
            pltpu.VMEM((total, latents), F32),
            pltpu.VMEM((total, latents), F32),
            pltpu.VMEM((total, latents), BF16),
            pltpu.VMEM((2 * rows, width), F32),
            pltpu.VMEM((half, rows, width), BF16),
            pltpu.VMEM((half, rows, width), BF16),
            pltpu.VMEM((half, rows, width), BF16),
            pltpu.VMEM((half, rows, width), BF16),
            pltpu.VMEM((total, width), BF16),
            pltpu.VMEM((total, latents), F32),
            pltpu.VMEM((total, latents), F32),
            pltpu.VMEM((total, latents), BF16),
            pltpu.VMEM((8, latents), F32),
            steps, steps, steps, steps, steps, steps, swap, swap, swap, swap,
            dma((2,)), dma((2,)), dma((4,)),
        ],
        compiler_params=pltpu.CompilerParams(
            collective_id=0, has_side_effects=True, vmem_limit_bytes=60 * MIB
        ),
        cost_estimate=pl.CostEstimate(
            flops=6 * total * width * latents, bytes_accessed=32 * MIB, transcendentals=0
        ),
    )(x, enc, enc_bias, dec, dec_bias, norm)


def enc_grad_kernel(full_ref, round_ref, out_ref):
    out_ref[...] = lax.dot_general(
        full_ref[...], round_ref[...], (((0,), (0,)), ((), ())), preferred_element_type=F32
    ).astype(BF16)


def enc_grad_call(full, rounded):
    total, width = full.shape
    latents = rounded.shape[1]
    tile = 512
    return pl.pallas_call(
        enc_grad_kernel,
        grid=(width // tile,),
        out_shape=jax.ShapeDtypeStruct((width, latents), BF16),
        in_specs=[
            pl.BlockSpec((total, tile), lambda i: (0, i)),
            pl.BlockSpec((total, latents), lambda i: (0, 0)),
        ],
        out_specs=pl.BlockSpec((tile, latents), lambda i: (i, 0)),
        compiler_params=pltpu.CompilerParams(vmem_limit_bytes=40 * MIB),
        cost_estimate=pl.CostEstimate(
            flops=2 * total * width * latents, bytes_accessed=13 * MIB, transcendentals=0
        ),
    )(full, rounded)


def dec_grad_kernel(scale, feat_ref, err_ref, dec_ref, norm_ref, out_ref):
    total, width = err_ref.shape
    chunk = 512
    feats = feat_ref[...].T
    sums = jnp.dot(feats, jnp.ones((total, 128), BF16), preferred_element_type=F32)[:, :1]
    factor = penalty_weight * scale * sums / norm_ref[...]
    for j in range(width // chunk):
        c = pl.ds(j * chunk, chunk)
        direct = jnp.dot(feats, err_ref[:, c], preferred_element_type=F32)
        out_ref[:, c] = (direct + factor * dec_ref[:, c].astype(F32)).astype(BF16)


def dec_grad_call(feat, err, dec, norm):
    total, width = err.shape
    latents = feat.shape[1]
    tile = 256
    scale = float(1.0 / (total ** 0.5))
    return pl.pallas_call(
        functools.partial(dec_grad_kernel, scale),
        grid=(latents // tile,),
        out_shape=jax.ShapeDtypeStruct((latents, width), BF16),
        in_specs=[
            pl.BlockSpec((total, tile), lambda i: (0, i)),
            pl.BlockSpec((total, width), lambda i: (0, 0)),
            pl.BlockSpec((tile, width), lambda i: (i, 0)),
            pl.BlockSpec((tile, 1), lambda i: (i, 0)),
        ],
        out_specs=pl.BlockSpec((tile, width), lambda i: (i, 0)),
        compiler_params=pltpu.CompilerParams(vmem_limit_bytes=40 * MIB),
        cost_estimate=pl.CostEstimate(
            flops=2 * total * width * latents, bytes_accessed=21 * MIB, transcendentals=0
        ),
    )(feat, err, dec, norm)


def per_device(n, streams, enc_weight, enc_bias, dec_weight, dec_bias):
    decoder = dec_weight[0]
    row_norm = jnp.sqrt(jnp.sum(jnp.square(decoder.astype(F32)), axis=1) + epsilon_sq)
    norm_rows = jnp.broadcast_to(row_norm[None, :], (8, row_norm.shape[0]))
    full, feat, err, rounded, enc_bias_grad, dec_bias_grad = main_call(
        n, streams[0], enc_weight[0], enc_bias[None, :], decoder, dec_bias, norm_rows
    )
    dec_grad = dec_grad_call(feat, err, decoder, row_norm[:, None])
    enc_grad = enc_grad_call(full, rounded)
    return (enc_grad[None], enc_bias_grad[0], dec_grad[None], dec_bias_grad)


def solution(mesh):
    in_specs = (
        P("layer", ("groups", "lat"), None),
        P(("groups", "layer"), None, "lat"),
        P(("groups", "lat")),
        P(("groups", "layer"), "lat", None),
        P(("groups", "layer"), "lat"),
    )
    out_specs = (
        P(("groups", "layer"), None, "lat"),
        P(("groups", "lat")),
        P(("groups", "layer"), "lat", None),
        P(("groups", "layer"), "lat"),
    )
    return jax.shard_map(
        functools.partial(per_device, mesh.shape["lat"]), mesh=mesh,
        in_specs=in_specs, out_specs=out_specs, check_vma=False,
    )
```

```python
import functools

import jax
import jax.numpy as jnp
from jax import lax
from jax.experimental import pallas as pl
from jax.experimental.pallas import tpu as pltpu
from jax.sharding import PartitionSpec as P

penalty_weight = 1.0
epsilon_sq = 1e-06
MESH = pl.DeviceIdType.MESH
MIB = 1024 * 1024
F32 = jnp.float32
BF16 = jnp.bfloat16


def ring_neighbours(n):
    index = lax.axis_index("lat")
    if n != 8:
        return lax.rem(index + 1, n), lax.rem(index + n - 1, n)
    half = n // 2

    def place_of(i):
        z, y = i // 2, lax.rem(i, 2)
        return jnp.where(y == 0, z, n - 1 - z)

    def index_of(p):
        return jnp.where(p < half, 2 * p, 2 * (n - 1 - p) + 1)

    place = place_of(index)
    return index_of(lax.rem(place + 1, n)), index_of(lax.rem(place + n - 1, n))


def step_kernel(
    n, x_ref, enc_hbm, enc_bias_ref, dec_hbm, dec_bias_ref,
    full_out, feat_out, err_out, round_out, norm_ref, bias_grad_ref, dec_bias_grad_ref,
    enc, dec, full, part, part_in, pre, feat, partial, sum_right, sum_left, in_right, in_left,
    err, grad, grad_in, rounded, norm_row, norm_in,
    g_send, g_recv, r_send, r_recv, e_send, e_recv, p_send, p_recv, q_send, q_recv, n_sem, w_sem, o_sem,
):
    rows, width = x_ref.shape
    latents = enc.shape[1]
    half = n // 2
    hw = width // 2
    total = n * rows
    scale = float(1.0 / (total ** 0.5))
    right, left = ring_neighbours(n)
    other = 1 - lax.axis_index("layer")
    lat = lax.axis_index("lat")
    to_right, to_left, to_other = {"lat": right}, {"lat": left}, {"layer": other}
    sending = []

    load_enc = pltpu.make_async_copy(enc_hbm, enc, w_sem.at[0])
    load_dec = pltpu.make_async_copy(dec_hbm, dec, w_sem.at[1])
    load_enc.start()
    load_dec.start()

    barrier = pltpu.get_barrier_semaphore()
    for target in (to_right, to_left, to_other):
        pl.semaphore_signal(barrier, inc=1, device_id=target, device_id_type=MESH)

    def slot_rows(slot, count=1):
        return pl.ds(slot * rows, count * rows)

    def send(src, dst, s_sem, r_sem, target):
        copy = pltpu.make_async_remote_copy(
            src_ref=src, dst_ref=dst, send_sem=s_sem, recv_sem=r_sem,
            device_id=target, device_id_type=MESH,
        )
        copy.start()
        sending.append(copy)
        return copy

    def step_span(d):
        if d == 0:
            return 0, 1
        if d == half:
            return n - 1, 1
        return 2 * d - 1, 2

    def gather(buf, s_sem, r_sem, consume):
        got = {}

        def forward(d, h, way):
            if d > half or (d == half and h != way):
                return
            if way == 0:
                src = 0 if d == 1 else 2 * d - 3
                dst = n - 1 if d == half else 2 * d - 1
            else:
                src = 2 * (d - 1)
                dst = n - 1 if d == half else 2 * d
            cols = pl.ds(h * hw, hw)
            got[(d, h, way)] = send(
                buf.at[slot_rows(src), cols], buf.at[slot_rows(dst), cols],
                s_sem.at[way, d - 1, h], r_sem.at[way, d - 1, h],
                to_right if way == 0 else to_left,
            )

        for order in range(2):
            for way in range(2):
                forward(1, (order + way) % 2, way)
        consume(0)
        for d in range(1, half + 1):
            for order in range(2):
                for way in range(2):
                    h = (order + way) % 2
                    if (d, h, way) in got:
                        got[(d, h, way)].wait_recv()
                        forward(d + 1, h, way)
            consume(d)

    full[slot_rows(0), :] = x_ref[...]
    pl.semaphore_wait(barrier, 3)

    tile = min(256, latents)
    swaps = {}

    def finish_pre(d):
        slot, count = step_span(d)
        swaps[d].wait_recv()

        @pl.loop(0, count * rows // 16)
        def _(i):
            r = pl.ds(pl.multiple_of(slot * rows + i * 16, 16), 16)
            value = part[r, :] + part_in[r, :] + enc_bias_ref[...]
            pre[r, :] = value
            soft = jnp.maximum(value, 0.0) + jnp.log1p(jnp.exp(-jnp.abs(value)))
            feat[r, :] = soft.astype(BF16)

    norm_swap = []

    def norms():
        load_dec.wait()

        @pl.loop(0, latents // 16)
        def _(i):
            r = pl.ds(pl.multiple_of(i * 16, 16), 16)
            value = jnp.square(dec[r, :].astype(F32))
            value = jnp.sqrt(jnp.sum(value, axis=1, keepdims=True) + epsilon_sq)
            norm_ref[r, :] = jnp.broadcast_to(value, (16, 128))

        for i in range(latents // 128):
            r = pl.ds(i * 128, 128)
            norm_row[:, r] = norm_ref[r, :].T[:8, :]
        norm_swap.append(send(norm_row, norm_in, n_sem.at[0], n_sem.at[1], to_other))

    def encode(d):
        if d == 0:
            load_enc.wait()
        slot, count = step_span(d)
        r = slot_rows(slot, count)

        @pl.loop(0, latents // tile)
        def _(j):
            c = pl.ds(pl.multiple_of(j * tile, tile), tile)
            part[r, c] = jnp.dot(full[r, :], enc[:, c], preferred_element_type=F32)

        swaps[d] = send(part.at[r, :], part_in.at[r, :], p_send.at[d], p_recv.at[d], to_other)
        if d >= 1:
            finish_pre(d - 1)
        if d == 1:
            norms()

    gather(full, g_send, g_recv, encode)
    save_full = pltpu.make_async_copy(full, full_out, o_sem.at[0])
    save_full.start()
    finish_pre(half)
    save_feat = pltpu.make_async_copy(feat, feat_out, o_sem.at[1])
    save_feat.start()

    wide = min(512, width)
    own = width // n

    def decode(d):
        slot, count = step_span(d)
        r = slot_rows(slot, count)
        to = pl.ds(0, count * rows)

        @pl.loop(0, width // wide)
        def _(j):
            c = pl.ds(pl.multiple_of(j * wide, wide), wide)
            partial[to, c] = jnp.dot(feat[r, :], dec[:, c], preferred_element_type=F32)

        mine = pl.ds(pl.multiple_of(lat * own, own), own)
        partial[to, mine] = partial[to, mine] + dec_bias_ref[...]

    def merge(source, base, arrived, index, target, h):
        @pl.loop(0, rows // 16)
        def _(i):
            r = pl.ds(pl.multiple_of(i * 16, 16), 16)
            c = pl.ds(h * hw, hw)
            value = source[pl.ds(pl.multiple_of(base + i * 16, 16), 16), c]
            if arrived is not None:
                value = value + arrived[index, r, c].astype(F32)
            target[r, c] = value.astype(target.dtype)

    moving = {}
    for d in range(half, 0, -1):
        decode(d)
        for order in range(2):
            for way in range(2):
                h = (order + way) % 2
                if d == half and h != way:
                    continue
                base = 0 if d == half or way == 1 else rows
                out = (sum_right, sum_left)[way]
                arrive = (in_right, in_left)[way]
                before = moving.get((d + 1, h, way))
                if before is not None:
                    before.wait_recv()
                merge(partial, base, None if before is None else arrive, d, out.at[d - 1], h)
                c = pl.ds(h * hw, hw)
                moving[(d, h, way)] = send(
                    out.at[d - 1, :, c], arrive.at[d - 1, :, c],
                    r_send.at[way, d - 1, h], r_recv.at[way, d - 1, h],
                    to_right if way == 0 else to_left,
                )
    decode(0)
    for order in range(2):
        for way in range(2):
            moving[(1, (order + way) % 2, way)].wait_recv()

    @pl.loop(0, rows // 16)
    def _(i):
        r = pl.ds(pl.multiple_of(i * 16, 16), 16)
        for h in range(2):
            c = pl.ds(h * hw, hw)
            recon = partial[r, c] + in_right[0, r, c].astype(F32) + in_left[0, r, c].astype(F32)
            err[r, c] = ((recon - x_ref[r, c].astype(F32)) * scale).astype(BF16)

    norm_swap[0].wait_recv()
    bias_grad_ref[...] = jnp.zeros_like(bias_grad_ref)
    grad_swaps = {}

    def finish_grad(d):
        slot, count = step_span(d)
        grad_swaps[d].wait_recv()

        @pl.loop(0, count * rows // 16)
        def _(i):
            r = pl.ds(pl.multiple_of(slot * rows + i * 16, 16), 16)
            strength = norm_row[0:1, :] + norm_in[0:1, :]
            value = grad[r, :] + grad_in[r, :] + (penalty_weight * scale) * strength
            value = value * jax.nn.sigmoid(pre[r, :])
            rounded[r, :] = value.astype(BF16)
            bias_grad_ref[...] += jnp.sum(value, axis=0, keepdims=True)

    def decode_grad(d):
        slot, count = step_span(d)
        r = slot_rows(slot, count)

        @pl.loop(0, latents // tile)
        def _(j):
            c = pl.ds(pl.multiple_of(j * tile, tile), tile)
            grad[r, c] = lax.dot_general(
                err[r, :], dec[c, :], (((1,), (1,)), ((), ())), preferred_element_type=F32
            )

        grad_swaps[d] = send(grad.at[r, :], grad_in.at[r, :], q_send.at[d], q_recv.at[d], to_other)
        if d >= 1:
            finish_grad(d - 1)

    gather(err, e_send, e_recv, decode_grad)
    save_err = pltpu.make_async_copy(err, err_out, o_sem.at[2])
    save_err.start()
    mine = pl.ds(pl.multiple_of(lat * own, own), own)
    dec_bias_grad_ref[...] = jnp.zeros_like(dec_bias_grad_ref)

    @pl.loop(0, total // 64)
    def _(i):
        r = pl.ds(pl.multiple_of(i * 64, 64), 64)
        dec_bias_grad_ref[...] += jnp.sum(err[r, mine].astype(F32), axis=0, keepdims=True)

    finish_grad(half)
    save_round = pltpu.make_async_copy(rounded, round_out, o_sem.at[3])
    save_round.start()
    for copy in sending:
        copy.wait_send()
    for save in (save_full, save_feat, save_err, save_round):
        save.wait()


def main_call(n, x, enc, enc_bias, dec, dec_bias):
    rows, width = x.shape
    latents = enc.shape[1]
    total = n * rows
    half = n // 2
    vmem = pl.BlockSpec(memory_space=pltpu.VMEM)
    hbm = pl.BlockSpec(memory_space=pl.ANY)
    dma = pltpu.SemaphoreType.DMA
    steps = dma((2, half, 2))
    swap = dma((half + 1,))
    return pl.pallas_call(
        functools.partial(step_kernel, n),
        out_shape=(
            jax.ShapeDtypeStruct((total, width), BF16),
            jax.ShapeDtypeStruct((total, latents), BF16),
            jax.ShapeDtypeStruct((total, width), BF16),
            jax.ShapeDtypeStruct((total, latents), BF16),
            jax.ShapeDtypeStruct((latents, 128), F32),
            jax.ShapeDtypeStruct((1, latents), F32),
            jax.ShapeDtypeStruct((1, width // n), F32),
        ),
        in_specs=[vmem, hbm, vmem, hbm, vmem],
        out_specs=(hbm, hbm, hbm, hbm, vmem, vmem, vmem),
        scratch_shapes=[
            pltpu.VMEM((width, latents), BF16),
            pltpu.VMEM((latents, width), BF16),
            pltpu.VMEM((total, width), BF16),
            pltpu.VMEM((total, latents), F32),
            pltpu.VMEM((total, latents), F32),
            pltpu.VMEM((total, latents), F32),
            pltpu.VMEM((total, latents), BF16),
            pltpu.VMEM((2 * rows, width), F32),
            pltpu.VMEM((half, rows, width), BF16),
            pltpu.VMEM((half, rows, width), BF16),
            pltpu.VMEM((half, rows, width), BF16),
            pltpu.VMEM((half, rows, width), BF16),
            pltpu.VMEM((total, width), BF16),
            pltpu.VMEM((total, latents), F32),
            pltpu.VMEM((total, latents), F32),
            pltpu.VMEM((total, latents), BF16),
            pltpu.VMEM((8, latents), F32),
            pltpu.VMEM((8, latents), F32),
            steps, steps, steps, steps, steps, steps, swap, swap, swap, swap,
            dma((2,)), dma((2,)), dma((4,)),
        ],
        compiler_params=pltpu.CompilerParams(
            collective_id=0, has_side_effects=True, vmem_limit_bytes=60 * MIB
        ),
        cost_estimate=pl.CostEstimate(
            flops=6 * total * width * latents, bytes_accessed=32 * MIB, transcendentals=0
        ),
    )(x, enc, enc_bias, dec, dec_bias)


def weight_grad_kernel(
    scale, full_ref, round_ref, feat_ref, err_ref, dec_ref, norm_ref, bias_grad_ref, dec_bias_grad_ref,
    enc_out, dec_out, bias_grad_out, dec_bias_grad_out, feats, factor,
):
    total = feat_ref.shape[0]
    latents, span = dec_ref.shape

    @pl.when(pl.program_id(0) == 0)
    def _():
        feats[...] = feat_ref[...].T
        sums = jnp.dot(feats[...], jnp.ones((total, 128), BF16), preferred_element_type=F32)
        factor[...] = penalty_weight * scale * sums / norm_ref[...]
        bias_grad_out[...] = bias_grad_ref[...]
        dec_bias_grad_out[...] = dec_bias_grad_ref[...]

    enc_out[...] = lax.dot_general(
        full_ref[...], round_ref[...], (((0,), (0,)), ((), ())), preferred_element_type=F32
    ).astype(BF16)
    step = min(256, latents)
    for j in range(latents // step):
        r = pl.ds(j * step, step)
        direct = jnp.dot(feats[r, :], err_ref[...], preferred_element_type=F32)
        shrink = factor[r, :1] * dec_ref[r, :].astype(F32)
        dec_out[r, :] = (direct + shrink).astype(BF16)


def weight_grad_call(full, rounded, feat, err, dec, norm, bias_grad, dec_bias_grad):
    total, width = full.shape
    latents = rounded.shape[1]
    own = dec_bias_grad.shape[1]
    tile = 512
    scale = float(1.0 / (total ** 0.5))

    def whole(rows, columns):
        return pl.BlockSpec((rows, columns), lambda i: (0, 0))

    def columns_of(rows):
        return pl.BlockSpec((rows, tile), lambda i: (0, i))

    return pl.pallas_call(
        functools.partial(weight_grad_kernel, scale),
        grid=(width // tile,),
        out_shape=(
            jax.ShapeDtypeStruct((width, latents), BF16),
            jax.ShapeDtypeStruct((latents, width), BF16),
            jax.ShapeDtypeStruct((1, latents), F32),
            jax.ShapeDtypeStruct((1, own), F32),
        ),
        in_specs=[
            columns_of(total), whole(total, latents), whole(total, latents), columns_of(total),
            columns_of(latents), whole(latents, 128), whole(1, latents), whole(1, own),
        ],
        out_specs=(
            pl.BlockSpec((tile, latents), lambda i: (i, 0)), columns_of(latents),
            whole(1, latents), whole(1, own),
        ),
        scratch_shapes=[pltpu.VMEM((latents, total), BF16), pltpu.VMEM((latents, 128), F32)],
        compiler_params=pltpu.CompilerParams(vmem_limit_bytes=60 * MIB),
        cost_estimate=pl.CostEstimate(
            flops=4 * total * width * latents, bytes_accessed=34 * MIB, transcendentals=0
        ),
    )(full, rounded, feat, err, dec, norm, bias_grad, dec_bias_grad)


def per_device(n, streams, enc_weight, enc_bias, dec_weight, dec_bias):
    decoder = dec_weight[0]
    full, feat, err, rounded, norm, bias_grad, dec_bias_grad = main_call(
        n, streams[0], enc_weight[0], enc_bias[None, :], decoder, dec_bias
    )
    enc_grad, dec_grad, bias_grad, dec_bias_grad = weight_grad_call(
        full, rounded, feat, err, decoder, norm, bias_grad, dec_bias_grad
    )
    return (enc_grad[None], bias_grad[0], dec_grad[None], dec_bias_grad)


def solution(mesh):
    in_specs = (
        P("layer", ("groups", "lat"), None),
        P(("groups", "layer"), None, "lat"),
        P(("groups", "lat")),
        P(("groups", "layer"), "lat", None),
        P(("groups", "layer"), "lat"),
    )
    out_specs = (
        P(("groups", "layer"), None, "lat"),
        P(("groups", "lat")),
        P(("groups", "layer"), "lat", None),
        P(("groups", "layer"), "lat"),
    )
    return jax.shard_map(
        functools.partial(per_device, mesh.shape["lat"]), mesh=mesh,
        in_specs=in_specs, out_specs=out_specs, check_vma=False,
    )
```

```python
import functools

import jax
import jax.numpy as jnp
from jax import lax
from jax.experimental import pallas as pl
from jax.experimental.pallas import tpu as pltpu
from jax.sharding import PartitionSpec as P

penalty_weight = 1.0
epsilon_sq = 1e-06
MESH = pl.DeviceIdType.MESH
MIB = 1024 * 1024
F32 = jnp.float32
BF16 = jnp.bfloat16


def ring_neighbours(n):
    index = lax.axis_index("lat")
    if n != 8:
        return lax.rem(index + 1, n), lax.rem(index + n - 1, n)
    half = n // 2

    def place_of(i):
        z, y = i // 2, lax.rem(i, 2)
        return jnp.where(y == 0, z, n - 1 - z)

    def index_of(p):
        return jnp.where(p < half, 2 * p, 2 * (n - 1 - p) + 1)

    place = place_of(index)
    return index_of(lax.rem(place + 1, n)), index_of(lax.rem(place + n - 1, n))


def step_kernel(
    n, x_ref, enc_hbm, enc_bias_ref, dec_hbm, dec_bias_ref,
    full_out, feat_out, err_out, round_out, norm_ref, bias_grad_ref, dec_bias_grad_ref,
    enc, dec, full, part, part_in, pre, feat, partial, sum_right, sum_left, in_right, in_left,
    err, grad, grad_in, rounded, norm_row, norm_in,
    g_send, g_recv, r_send, r_recv, e_send, e_recv, p_send, p_recv, q_send, q_recv, n_sem, w_sem, o_sem, s_sem,
):
    rows, width = x_ref.shape
    latents = enc.shape[1]
    half = n // 2
    hw = width // 2
    total = n * rows
    scale = float(1.0 / (total ** 0.5))
    right, left = ring_neighbours(n)
    other = 1 - lax.axis_index("layer")
    lat = lax.axis_index("lat")
    to_right, to_left, to_other = {"lat": right}, {"lat": left}, {"layer": other}
    sending = []

    load_enc = pltpu.make_async_copy(enc_hbm, enc, w_sem.at[0])
    load_dec = pltpu.make_async_copy(dec_hbm, dec, w_sem.at[1])
    load_enc.start()
    load_dec.start()

    barrier = pltpu.get_barrier_semaphore()
    for target in (to_right, to_left, to_other):
        pl.semaphore_signal(barrier, inc=1, device_id=target, device_id_type=MESH)

    def slot_rows(slot, count=1):
        return pl.ds(slot * rows, count * rows)

    def send(src, dst, s_sem, r_sem, target):
        copy = pltpu.make_async_remote_copy(
            src_ref=src, dst_ref=dst, send_sem=s_sem, recv_sem=r_sem,
            device_id=target, device_id_type=MESH,
        )
        copy.start()
        sending.append(copy)
        return copy

    def step_span(d):
        if d == 0:
            return 0, 1
        if d == half:
            return n - 1, 1
        return 2 * d - 1, 2

    def gather(buf, out_sem, in_sem, consume):
        got = {}

        def forward(d, h, way):
            if d > half or (d == half and h != way):
                return
            if way == 0:
                src = 0 if d == 1 else 2 * d - 3
                dst = n - 1 if d == half else 2 * d - 1
            else:
                src = 2 * (d - 1)
                dst = n - 1 if d == half else 2 * d
            cols = pl.ds(h * hw, hw)
            got[(d, h, way)] = send(
                buf.at[slot_rows(src), cols], buf.at[slot_rows(dst), cols],
                out_sem.at[way, d - 1, h], in_sem.at[way, d - 1, h],
                to_right if way == 0 else to_left,
            )

        for order in range(2):
            for way in range(2):
                forward(1, (order + way) % 2, way)
        consume(0)
        for d in range(1, half + 1):
            for order in range(2):
                for way in range(2):
                    h = (order + way) % 2
                    if (d, h, way) in got:
                        got[(d, h, way)].wait_recv()
                        forward(d + 1, h, way)
            consume(d)

    full[slot_rows(0), :] = x_ref[...]
    pl.semaphore_wait(barrier, 3)

    tile = min(256, latents)
    swaps = {}

    def finish_pre(d):
        slot, count = step_span(d)
        swaps[d].wait_recv()

        @pl.loop(0, count * rows // 16)
        def _(i):
            r = pl.ds(pl.multiple_of(slot * rows + i * 16, 16), 16)
            value = part[r, :] + part_in[r, :] + enc_bias_ref[...]
            pre[r, :] = value
            soft = jnp.maximum(value, 0.0) + jnp.log1p(jnp.exp(-jnp.abs(value)))
            feat[r, :] = soft.astype(BF16)

    norm_swap = []

    def norms():
        load_dec.wait()

        @pl.loop(0, latents // 16)
        def _(i):
            r = pl.ds(pl.multiple_of(i * 16, 16), 16)
            value = jnp.square(dec[r, :].astype(F32))
            value = jnp.sqrt(jnp.sum(value, axis=1, keepdims=True) + epsilon_sq)
            norm_ref[r, :] = jnp.broadcast_to(value, (16, 128))

        for i in range(latents // 128):
            r = pl.ds(i * 128, 128)
            norm_row[:, r] = norm_ref[r, :].T[:8, :]
        norm_swap.append(send(norm_row, norm_in, n_sem.at[0], n_sem.at[1], to_other))

    def encode(d):
        if d == 0:
            load_enc.wait()
        slot, count = step_span(d)
        r = slot_rows(slot, count)

        @pl.loop(0, latents // tile)
        def _(j):
            c = pl.ds(pl.multiple_of(j * tile, tile), tile)
            part[r, c] = jnp.dot(full[r, :], enc[:, c], preferred_element_type=F32)

        swaps[d] = send(part.at[r, :], part_in.at[r, :], p_send.at[d], p_recv.at[d], to_other)
        if d >= 1:
            finish_pre(d - 1)
        if d == 1:
            norms()

    gather(full, g_send, g_recv, encode)
    save_full = pltpu.make_async_copy(full, full_out, o_sem.at[0])
    save_full.start()
    finish_pre(half)
    save_feat = pltpu.make_async_copy(feat, feat_out, o_sem.at[1])
    save_feat.start()

    wide = min(512, width)
    own = width // n

    def decode(d):
        slot, count = step_span(d)
        r = slot_rows(slot, count)
        to = pl.ds(0, count * rows)

        @pl.loop(0, width // wide)
        def _(j):
            c = pl.ds(pl.multiple_of(j * wide, wide), wide)
            partial[to, c] = jnp.dot(feat[r, :], dec[:, c], preferred_element_type=F32)

        mine = pl.ds(pl.multiple_of(lat * own, own), own)
        partial[to, mine] = partial[to, mine] + dec_bias_ref[...]

    def merge(source, base, arrived, index, target, h):
        @pl.loop(0, rows // 16)
        def _(i):
            r = pl.ds(pl.multiple_of(i * 16, 16), 16)
            c = pl.ds(h * hw, hw)
            value = source[pl.ds(pl.multiple_of(base + i * 16, 16), 16), c]
            if arrived is not None:
                value = value + arrived[index, r, c].astype(F32)
            target[r, c] = value.astype(target.dtype)

    moving = {}
    for d in range(half, 0, -1):
        decode(d)
        for order in range(2):
            for way in range(2):
                h = (order + way + 1) % 2
                if d == half and h != way:
                    continue
                base = 0 if d == half or way == 1 else rows
                out = (sum_right, sum_left)[way]
                arrive = (in_right, in_left)[way]
                before = moving.get((d + 1, h, way))
                if before is not None:
                    before.wait_recv()
                merge(partial, base, None if before is None else arrive, d, out.at[d - 1], h)
                c = pl.ds(h * hw, hw)
                moving[(d, h, way)] = send(
                    out.at[d - 1, :, c], arrive.at[d - 1, :, c],
                    r_send.at[way, d - 1, h], r_recv.at[way, d - 1, h],
                    to_right if way == 0 else to_left,
                )
    decode(0)
    for order in range(2):
        for way in range(2):
            moving[(1, (order + way + 1) % 2, way)].wait_recv()

    @pl.loop(0, rows // 16)
    def _(i):
        r = pl.ds(pl.multiple_of(i * 16, 16), 16)
        for h in range(2):
            c = pl.ds(h * hw, hw)
            recon = partial[r, c] + in_right[0, r, c].astype(F32) + in_left[0, r, c].astype(F32)
            err[r, c] = ((recon - x_ref[r, c].astype(F32)) * scale).astype(BF16)

    norm_swap[0].wait_recv()
    bias_grad_ref[...] = jnp.zeros_like(bias_grad_ref)
    dec_bias_grad_ref[...] = jnp.zeros_like(dec_bias_grad_ref)
    grad_swaps = {}
    saves = []

    def save_step(buf, out, d, which):
        r = slot_rows(*step_span(d))
        copy = pltpu.make_async_copy(buf.at[r, :], out.at[r, :], s_sem.at[which, d])
        copy.start()
        saves.append(copy)

    def finish_grad(d):
        slot, count = step_span(d)
        grad_swaps[d].wait_recv()

        @pl.loop(0, count * rows // 16)
        def _(i):
            r = pl.ds(pl.multiple_of(slot * rows + i * 16, 16), 16)
            strength = norm_row[0:1, :] + norm_in[0:1, :]
            value = grad[r, :] + grad_in[r, :] + (penalty_weight * scale) * strength
            value = value * jax.nn.sigmoid(pre[r, :])
            rounded[r, :] = value.astype(BF16)
            bias_grad_ref[...] += jnp.sum(value, axis=0, keepdims=True)

        save_step(rounded, round_out, d, 1)

    def decode_grad(d):
        slot, count = step_span(d)
        r = slot_rows(slot, count)

        @pl.loop(0, latents // tile)
        def _(j):
            c = pl.ds(pl.multiple_of(j * tile, tile), tile)
            grad[r, c] = lax.dot_general(
                err[r, :], dec[c, :], (((1,), (1,)), ((), ())), preferred_element_type=F32
            )

        grad_swaps[d] = send(grad.at[r, :], grad_in.at[r, :], q_send.at[d], q_recv.at[d], to_other)
        save_step(err, err_out, d, 0)
        mine = pl.ds(pl.multiple_of(lat * own, own), own)

        @pl.loop(0, count * rows // 16)
        def _(i):
            block = pl.ds(pl.multiple_of(slot * rows + i * 16, 16), 16)
            dec_bias_grad_ref[...] += jnp.sum(err[block, mine].astype(F32), axis=0, keepdims=True)

        if d >= 1:
            finish_grad(d - 1)

    gather(err, e_send, e_recv, decode_grad)
    finish_grad(half)
    for copy in sending:
        copy.wait_send()
    for save in [save_full, save_feat] + saves:
        save.wait()


def main_call(n, x, enc, enc_bias, dec, dec_bias):
    rows, width = x.shape
    latents = enc.shape[1]
    total = n * rows
    half = n // 2
    vmem = pl.BlockSpec(memory_space=pltpu.VMEM)
    hbm = pl.BlockSpec(memory_space=pl.ANY)
    dma = pltpu.SemaphoreType.DMA
    steps = dma((2, half, 2))
    swap = dma((half + 1,))
    return pl.pallas_call(
        functools.partial(step_kernel, n),
        out_shape=(
            jax.ShapeDtypeStruct((total, width), BF16),
            jax.ShapeDtypeStruct((total, latents), BF16),
            jax.ShapeDtypeStruct((total, width), BF16),
            jax.ShapeDtypeStruct((total, latents), BF16),
            jax.ShapeDtypeStruct((latents, 128), F32),
            jax.ShapeDtypeStruct((1, latents), F32),
            jax.ShapeDtypeStruct((1, width // n), F32),
        ),
        in_specs=[vmem, hbm, vmem, hbm, vmem],
        out_specs=(hbm, hbm, hbm, hbm, vmem, vmem, vmem),
        scratch_shapes=[
            pltpu.VMEM((width, latents), BF16),
            pltpu.VMEM((latents, width), BF16),
            pltpu.VMEM((total, width), BF16),
            pltpu.VMEM((total, latents), F32),
            pltpu.VMEM((total, latents), F32),
            pltpu.VMEM((total, latents), F32),
            pltpu.VMEM((total, latents), BF16),
            pltpu.VMEM((2 * rows, width), F32),
            pltpu.VMEM((half, rows, width), BF16),
            pltpu.VMEM((half, rows, width), BF16),
            pltpu.VMEM((half, rows, width), BF16),
            pltpu.VMEM((half, rows, width), BF16),
            pltpu.VMEM((total, width), BF16),
            pltpu.VMEM((total, latents), F32),
            pltpu.VMEM((total, latents), F32),
            pltpu.VMEM((total, latents), BF16),
            pltpu.VMEM((8, latents), F32),
            pltpu.VMEM((8, latents), F32),
            steps, steps, steps, steps, steps, steps, swap, swap, swap, swap,
            dma((2,)), dma((2,)), dma((2,)), dma((2, half + 1)),
        ],
        compiler_params=pltpu.CompilerParams(
            collective_id=0, has_side_effects=True, vmem_limit_bytes=60 * MIB
        ),
        cost_estimate=pl.CostEstimate(
            flops=6 * total * width * latents, bytes_accessed=32 * MIB, transcendentals=0
        ),
    )(x, enc, enc_bias, dec, dec_bias)


def weight_grad_kernel(
    scale, full_ref, round_ref, feat_ref, err_ref, dec_ref, norm_ref, bias_grad_ref, dec_bias_grad_ref,
    enc_out, dec_out, bias_grad_out, dec_bias_grad_out,
):
    total = feat_ref.shape[0]
    width = err_ref.shape[1]

    @pl.when(pl.program_id(0) == 0)
    def _():
        bias_grad_out[...] = bias_grad_ref[...]
        dec_bias_grad_out[...] = dec_bias_grad_ref[...]

    enc_out[...] = lax.dot_general(
        full_ref[...], round_ref[...], (((0,), (0,)), ((), ())), preferred_element_type=F32
    ).astype(BF16)
    feats = feat_ref[...].T
    sums = jnp.dot(feats, jnp.ones((total, 128), BF16), preferred_element_type=F32)
    factor = (penalty_weight * scale * sums / norm_ref[...])[:, :1]
    step = min(1024, width)
    for j in range(width // step):
        c = pl.ds(j * step, step)
        direct = jnp.dot(feats, err_ref[:, c], preferred_element_type=F32)
        dec_out[:, c] = (direct + factor * dec_ref[:, c].astype(F32)).astype(BF16)


def weight_grad_call(full, rounded, feat, err, dec, norm, bias_grad, dec_bias_grad):
    total, width = full.shape
    latents = rounded.shape[1]
    own = dec_bias_grad.shape[1]
    steps = min(4, latents // 128)
    wide, tall = width // steps, latents // steps
    scale = float(1.0 / (total ** 0.5))

    def whole(rows, columns):
        return pl.BlockSpec((rows, columns), lambda i: (0, 0))

    def columns_of(rows, columns):
        return pl.BlockSpec((rows, columns), lambda i: (0, i))

    def rows_of(rows, columns):
        return pl.BlockSpec((rows, columns), lambda i: (i, 0))

    return pl.pallas_call(
        functools.partial(weight_grad_kernel, scale),
        grid=(steps,),
        out_shape=(
            jax.ShapeDtypeStruct((width, latents), BF16),
            jax.ShapeDtypeStruct((latents, width), BF16),
            jax.ShapeDtypeStruct((1, latents), F32),
            jax.ShapeDtypeStruct((1, own), F32),
        ),
        in_specs=[
            columns_of(total, wide), whole(total, latents), columns_of(total, tall), whole(total, width),
            rows_of(tall, width), rows_of(tall, 128), whole(1, latents), whole(1, own),
        ],
        out_specs=(
            rows_of(wide, latents), rows_of(tall, width),
            whole(1, latents), whole(1, own),
        ),
        compiler_params=pltpu.CompilerParams(vmem_limit_bytes=60 * MIB),
        cost_estimate=pl.CostEstimate(
            flops=4 * total * width * latents, bytes_accessed=34 * MIB, transcendentals=0
        ),
    )(full, rounded, feat, err, dec, norm, bias_grad, dec_bias_grad)


def per_device(n, streams, enc_weight, enc_bias, dec_weight, dec_bias):
    decoder = dec_weight[0]
    full, feat, err, rounded, norm, bias_grad, dec_bias_grad = main_call(
        n, streams[0], enc_weight[0], enc_bias[None, :], decoder, dec_bias
    )
    enc_grad, dec_grad, bias_grad, dec_bias_grad = weight_grad_call(
        full, rounded, feat, err, decoder, norm, bias_grad, dec_bias_grad
    )
    return (enc_grad[None], bias_grad[0], dec_grad[None], dec_bias_grad)


def solution(mesh):
    in_specs = (
        P("layer", ("groups", "lat"), None),
        P(("groups", "layer"), None, "lat"),
        P(("groups", "lat")),
        P(("groups", "layer"), "lat", None),
        P(("groups", "layer"), "lat"),
    )
    out_specs = (
        P(("groups", "layer"), None, "lat"),
        P(("groups", "lat")),
        P(("groups", "layer"), "lat", None),
        P(("groups", "layer"), "lat"),
    )
    return jax.shard_map(
        functools.partial(per_device, mesh.shape["lat"]), mesh=mesh,
        in_specs=in_specs, out_specs=out_specs, check_vma=False,
    )
```

```python
import functools

import jax
import jax.numpy as jnp
from jax import lax
from jax.experimental import pallas as pl
from jax.experimental.pallas import tpu as pltpu
from jax.sharding import PartitionSpec as P

penalty_weight = 1.0
epsilon_sq = 1e-06
MESH = pl.DeviceIdType.MESH
MIB = 1024 * 1024
F32 = jnp.float32
BF16 = jnp.bfloat16


def ring_neighbours(n):
    index = lax.axis_index("lat")
    if n != 8:
        return lax.rem(index + 1, n), lax.rem(index + n - 1, n)
    half = n // 2

    def place_of(i):
        z, y = i // 2, lax.rem(i, 2)
        return jnp.where(y == 0, z, n - 1 - z)

    def index_of(p):
        return jnp.where(p < half, 2 * p, 2 * (n - 1 - p) + 1)

    place = place_of(index)
    return index_of(lax.rem(place + 1, n)), index_of(lax.rem(place + n - 1, n))


def step_kernel(
    n, x_ref, enc_hbm, enc_bias_ref, dec_hbm, dec_bias_ref,
    full_out, feat_out, err_out, round_out, norm_ref, bias_grad_ref, dec_bias_grad_ref,
    enc, dec, full, part, part_in, pre, feat, partial, sum_right, sum_left, in_right, in_left,
    err, grad, grad_in, rounded, norm_row, norm_in,
    g_send, g_recv, r_send, r_recv, e_send, e_recv, p_send, p_recv, q_send, q_recv, n_sem, w_sem, o_sem, s_sem,
):
    rows, width = x_ref.shape
    latents = enc.shape[1]
    half = n // 2
    hw = width // 2
    total = n * rows
    scale = float(1.0 / (total ** 0.5))
    right, left = ring_neighbours(n)
    other = 1 - lax.axis_index("layer")
    lat = lax.axis_index("lat")
    to_right, to_left, to_other = {"lat": right}, {"lat": left}, {"layer": other}
    sending = []

    load_enc = pltpu.make_async_copy(enc_hbm, enc, w_sem.at[0])
    load_dec = pltpu.make_async_copy(dec_hbm, dec, w_sem.at[1])
    load_enc.start()
    load_dec.start()

    barrier = pltpu.get_barrier_semaphore()
    for target in (to_right, to_left, to_other):
        pl.semaphore_signal(barrier, inc=1, device_id=target, device_id_type=MESH)

    def slot_rows(slot, count=1):
        return pl.ds(slot * rows, count * rows)

    def send(src, dst, s_sem, r_sem, target):
        copy = pltpu.make_async_remote_copy(
            src_ref=src, dst_ref=dst, send_sem=s_sem, recv_sem=r_sem,
            device_id=target, device_id_type=MESH,
        )
        copy.start()
        sending.append(copy)
        return copy

    def step_span(d):
        if d == 0:
            return 0, 1
        if d == half:
            return n - 1, 1
        return 2 * d - 1, 2

    def gather(buf, out_sem, in_sem, consume):
        got = {}

        def forward(d, h, way):
            if d > half or (d == half and h != way):
                return
            if way == 0:
                src = 0 if d == 1 else 2 * d - 3
                dst = n - 1 if d == half else 2 * d - 1
            else:
                src = 2 * (d - 1)
                dst = n - 1 if d == half else 2 * d
            cols = pl.ds(h * hw, hw)
            got[(d, h, way)] = send(
                buf.at[slot_rows(src), cols], buf.at[slot_rows(dst), cols],
                out_sem.at[way, d - 1, h], in_sem.at[way, d - 1, h],
                to_right if way == 0 else to_left,
            )

        for order in range(2):
            for way in range(2):
                forward(1, (order + way) % 2, way)
        consume(0)
        for d in range(1, half + 1):
            for order in range(2):
                for way in range(2):
                    h = (order + way) % 2
                    if (d, h, way) in got:
                        got[(d, h, way)].wait_recv()
                        forward(d + 1, h, way)
            consume(d)

    full[slot_rows(0), :] = x_ref[...]
    pl.semaphore_wait(barrier, 3)

    tile = min(256, latents)
    swaps = {}

    def finish_pre(d):
        slot, count = step_span(d)
        swaps[d].wait_recv()

        @pl.loop(0, count * rows // 16)
        def _(i):
            r = pl.ds(pl.multiple_of(slot * rows + i * 16, 16), 16)
            value = part[r, :] + part_in[r, :] + enc_bias_ref[...]
            pre[r, :] = value
            soft = jnp.maximum(value, 0.0) + jnp.log1p(jnp.exp(-jnp.abs(value)))
            feat[r, :] = soft.astype(BF16)

    norm_swap = []

    def norms():
        load_dec.wait()

        @pl.loop(0, latents // 16)
        def _(i):
            r = pl.ds(pl.multiple_of(i * 16, 16), 16)
            value = jnp.square(dec[r, :].astype(F32))
            value = jnp.sqrt(jnp.sum(value, axis=1, keepdims=True) + epsilon_sq)
            norm_ref[r, :] = jnp.broadcast_to(value, (16, 128))

        for i in range(latents // 128):
            r = pl.ds(i * 128, 128)
            norm_row[:, r] = norm_ref[r, :].T[:8, :]
        norm_swap.append(send(norm_row, norm_in, n_sem.at[0], n_sem.at[1], to_other))

    def encode(d):
        if d == 0:
            load_enc.wait()
        slot, count = step_span(d)
        r = slot_rows(slot, count)

        @pl.loop(0, latents // tile, unroll=True)
        def _(j):
            c = pl.ds(pl.multiple_of(j * tile, tile), tile)
            part[r, c] = jnp.dot(full[r, :], enc[:, c], preferred_element_type=F32)

        swaps[d] = send(part.at[r, :], part_in.at[r, :], p_send.at[d], p_recv.at[d], to_other)
        if d >= 1:
            finish_pre(d - 1)
        if d == 1:
            norms()

    gather(full, g_send, g_recv, encode)
    save_full = pltpu.make_async_copy(full, full_out, o_sem.at[0])
    save_full.start()
    finish_pre(half)
    save_feat = pltpu.make_async_copy(feat, feat_out, o_sem.at[1])
    save_feat.start()

    wide = min(512, width)
    own = width // n

    def decode(d):
        slot, count = step_span(d)
        r = slot_rows(slot, count)
        to = pl.ds(0, count * rows)

        @pl.loop(0, width // wide, unroll=2)
        def _(j):
            c = pl.ds(pl.multiple_of(j * wide, wide), wide)
            partial[to, c] = jnp.dot(feat[r, :], dec[:, c], preferred_element_type=F32)

        mine = pl.ds(pl.multiple_of(lat * own, own), own)
        partial[to, mine] = partial[to, mine] + dec_bias_ref[...]

    def merge(source, base, arrived, index, target, h):
        @pl.loop(0, rows // 16)
        def _(i):
            r = pl.ds(pl.multiple_of(i * 16, 16), 16)
            c = pl.ds(h * hw, hw)
            value = source[pl.ds(pl.multiple_of(base + i * 16, 16), 16), c]
            if arrived is not None:
                value = value + arrived[index, r, c].astype(F32)
            target[r, c] = value.astype(target.dtype)

    moving = {}
    for d in range(half, 0, -1):
        decode(d)
        for order in range(2):
            for way in range(2):
                h = (order + way + 1) % 2
                if d == half and h != way:
                    continue
                base = 0 if d == half or way == 1 else rows
                out = (sum_right, sum_left)[way]
                arrive = (in_right, in_left)[way]
                before = moving.get((d + 1, h, way))
                if before is not None:
                    before.wait_recv()
                merge(partial, base, None if before is None else arrive, d, out.at[d - 1], h)
                c = pl.ds(h * hw, hw)
                moving[(d, h, way)] = send(
                    out.at[d - 1, :, c], arrive.at[d - 1, :, c],
                    r_send.at[way, d - 1, h], r_recv.at[way, d - 1, h],
                    to_right if way == 0 else to_left,
                )
    decode(0)
    for order in range(2):
        for way in range(2):
            moving[(1, (order + way + 1) % 2, way)].wait_recv()

    @pl.loop(0, rows // 16)
    def _(i):
        r = pl.ds(pl.multiple_of(i * 16, 16), 16)
        for h in range(2):
            c = pl.ds(h * hw, hw)
            recon = partial[r, c] + in_right[0, r, c].astype(F32) + in_left[0, r, c].astype(F32)
            err[r, c] = ((recon - x_ref[r, c].astype(F32)) * scale).astype(BF16)

    norm_swap[0].wait_recv()
    bias_grad_ref[...] = jnp.zeros_like(bias_grad_ref)
    dec_bias_grad_ref[...] = jnp.zeros_like(dec_bias_grad_ref)
    grad_swaps = {}
    saves = []

    def save_step(buf, out, d, which):
        r = slot_rows(*step_span(d))
        copy = pltpu.make_async_copy(buf.at[r, :], out.at[r, :], s_sem.at[which, d])
        copy.start()
        saves.append(copy)

    def finish_grad(d):
        slot, count = step_span(d)
        grad_swaps[d].wait_recv()

        @pl.loop(0, count * rows // 16)
        def _(i):
            r = pl.ds(pl.multiple_of(slot * rows + i * 16, 16), 16)
            strength = norm_row[0:1, :] + norm_in[0:1, :]
            value = grad[r, :] + grad_in[r, :] + (penalty_weight * scale) * strength
            value = value * jax.nn.sigmoid(pre[r, :])
            rounded[r, :] = value.astype(BF16)
            bias_grad_ref[...] += jnp.sum(value, axis=0, keepdims=True)

        save_step(rounded, round_out, d, 1)

    def decode_grad(d):
        slot, count = step_span(d)
        r = slot_rows(slot, count)

        @pl.loop(0, latents // tile, unroll=True)
        def _(j):
            c = pl.ds(pl.multiple_of(j * tile, tile), tile)
            grad[r, c] = lax.dot_general(
                err[r, :], dec[c, :], (((1,), (1,)), ((), ())), preferred_element_type=F32
            )

        grad_swaps[d] = send(grad.at[r, :], grad_in.at[r, :], q_send.at[d], q_recv.at[d], to_other)
        save_step(err, err_out, d, 0)
        mine = pl.ds(pl.multiple_of(lat * own, own), own)

        @pl.loop(0, count * rows // 16)
        def _(i):
            block = pl.ds(pl.multiple_of(slot * rows + i * 16, 16), 16)
            dec_bias_grad_ref[...] += jnp.sum(err[block, mine].astype(F32), axis=0, keepdims=True)

        if d >= 1:
            finish_grad(d - 1)

    gather(err, e_send, e_recv, decode_grad)
    finish_grad(half)
    for copy in sending:
        copy.wait_send()
    for save in [save_full, save_feat] + saves:
        save.wait()


def main_call(n, x, enc, enc_bias, dec, dec_bias):
    rows, width = x.shape
    latents = enc.shape[1]
    total = n * rows
    half = n // 2
    vmem = pl.BlockSpec(memory_space=pltpu.VMEM)
    hbm = pl.BlockSpec(memory_space=pl.ANY)
    dma = pltpu.SemaphoreType.DMA
    steps = dma((2, half, 2))
    swap = dma((half + 1,))
    return pl.pallas_call(
        functools.partial(step_kernel, n),
        out_shape=(
            jax.ShapeDtypeStruct((total, width), BF16),
            jax.ShapeDtypeStruct((total, latents), BF16),
            jax.ShapeDtypeStruct((total, width), BF16),
            jax.ShapeDtypeStruct((total, latents), BF16),
            jax.ShapeDtypeStruct((latents, 128), F32),
            jax.ShapeDtypeStruct((1, latents), F32),
            jax.ShapeDtypeStruct((1, width // n), F32),
        ),
        in_specs=[vmem, hbm, vmem, hbm, vmem],
        out_specs=(hbm, hbm, hbm, hbm, vmem, vmem, vmem),
        scratch_shapes=[
            pltpu.VMEM((width, latents), BF16),
            pltpu.VMEM((latents, width), BF16),
            pltpu.VMEM((total, width), BF16),
            pltpu.VMEM((total, latents), F32),
            pltpu.VMEM((total, latents), F32),
            pltpu.VMEM((total, latents), F32),
            pltpu.VMEM((total, latents), BF16),
            pltpu.VMEM((2 * rows, width), F32),
            pltpu.VMEM((half, rows, width), BF16),
            pltpu.VMEM((half, rows, width), BF16),
            pltpu.VMEM((half, rows, width), BF16),
            pltpu.VMEM((half, rows, width), BF16),
            pltpu.VMEM((total, width), BF16),
            pltpu.VMEM((total, latents), F32),
            pltpu.VMEM((total, latents), F32),
            pltpu.VMEM((total, latents), BF16),
            pltpu.VMEM((8, latents), F32),
            pltpu.VMEM((8, latents), F32),
            steps, steps, steps, steps, steps, steps, swap, swap, swap, swap,
            dma((2,)), dma((2,)), dma((2,)), dma((2, half + 1)),
        ],
        compiler_params=pltpu.CompilerParams(
            collective_id=0, has_side_effects=True, vmem_limit_bytes=60 * MIB
        ),
        cost_estimate=pl.CostEstimate(
            flops=6 * total * width * latents, bytes_accessed=32 * MIB, transcendentals=0
        ),
    )(x, enc, enc_bias, dec, dec_bias)


def weight_grad_kernel(
    scale, full_ref, round_ref, feat_ref, err_ref, dec_ref, norm_ref, bias_grad_ref, dec_bias_grad_ref,
    enc_out, dec_out, bias_grad_out, dec_bias_grad_out,
):
    total = feat_ref.shape[0]
    width = err_ref.shape[1]

    @pl.when(pl.program_id(0) == 0)
    def _():
        bias_grad_out[...] = bias_grad_ref[...]
        dec_bias_grad_out[...] = dec_bias_grad_ref[...]

    enc_out[...] = lax.dot_general(
        full_ref[...], round_ref[...], (((0,), (0,)), ((), ())), preferred_element_type=F32
    ).astype(BF16)
    feats = feat_ref[...].T
    sums = jnp.dot(feats, jnp.ones((total, 128), BF16), preferred_element_type=F32)
    factor = (penalty_weight * scale * sums / norm_ref[...])[:, :1]
    step = min(1024, width)
    for j in range(width // step):
        c = pl.ds(j * step, step)
        direct = jnp.dot(feats, err_ref[:, c], preferred_element_type=F32)
        dec_out[:, c] = (direct + factor * dec_ref[:, c].astype(F32)).astype(BF16)


def weight_grad_call(full, rounded, feat, err, dec, norm, bias_grad, dec_bias_grad):
    total, width = full.shape
    latents = rounded.shape[1]
    own = dec_bias_grad.shape[1]
    steps = min(4, latents // 128)
    wide, tall = width // steps, latents // steps
    scale = float(1.0 / (total ** 0.5))

    def whole(rows, columns):
        return pl.BlockSpec((rows, columns), lambda i: (0, 0))

    def columns_of(rows, columns):
        return pl.BlockSpec((rows, columns), lambda i: (0, i))

    def rows_of(rows, columns):
        return pl.BlockSpec((rows, columns), lambda i: (i, 0))

    return pl.pallas_call(
        functools.partial(weight_grad_kernel, scale),
        grid=(steps,),
        out_shape=(
            jax.ShapeDtypeStruct((width, latents), BF16),
            jax.ShapeDtypeStruct((latents, width), BF16),
            jax.ShapeDtypeStruct((1, latents), F32),
            jax.ShapeDtypeStruct((1, own), F32),
        ),
        in_specs=[
            columns_of(total, wide), whole(total, latents), columns_of(total, tall), whole(total, width),
            rows_of(tall, width), rows_of(tall, 128), whole(1, latents), whole(1, own),
        ],
        out_specs=(
            rows_of(wide, latents), rows_of(tall, width),
            whole(1, latents), whole(1, own),
        ),
        compiler_params=pltpu.CompilerParams(vmem_limit_bytes=60 * MIB),
        cost_estimate=pl.CostEstimate(
            flops=4 * total * width * latents, bytes_accessed=34 * MIB, transcendentals=0
        ),
    )(full, rounded, feat, err, dec, norm, bias_grad, dec_bias_grad)


def per_device(n, streams, enc_weight, enc_bias, dec_weight, dec_bias):
    decoder = dec_weight[0]
    full, feat, err, rounded, norm, bias_grad, dec_bias_grad = main_call(
        n, streams[0], enc_weight[0], enc_bias[None, :], decoder, dec_bias
    )
    enc_grad, dec_grad, bias_grad, dec_bias_grad = weight_grad_call(
        full, rounded, feat, err, decoder, norm, bias_grad, dec_bias_grad
    )
    return (enc_grad[None], bias_grad[0], dec_grad[None], dec_bias_grad)


def solution(mesh):
    in_specs = (
        P("layer", ("groups", "lat"), None),
        P(("groups", "layer"), None, "lat"),
        P(("groups", "lat")),
        P(("groups", "layer"), "lat", None),
        P(("groups", "layer"), "lat"),
    )
    out_specs = (
        P(("groups", "layer"), None, "lat"),
        P(("groups", "lat")),
        P(("groups", "layer"), "lat", None),
        P(("groups", "layer"), "lat"),
    )
    return jax.shard_map(
        functools.partial(per_device, mesh.shape["lat"]), mesh=mesh,
        in_specs=in_specs, out_specs=out_specs, check_vma=False,
    )
```
